32 devices in a mesh: dp: 8 (over z, y), tensor: 4 (over x, core).
Axes of the slice: x: 2, y: 2, z: 4, core: 2. Of those that a mesh axis runs over, the one named last changes fastest.
Arguments:
- inputs: bfloat16 [8192, 1024], P('dp'), may hold values from -6 to 6
- memory: bfloat16 [8192, 1024], P('dp'), may hold values from -6 to 6
- prefix: int32 [8], P('dp'), may hold values from 102 to 512, as said below
- self_qkv: bfloat16 [3, 1024, 1024], P(None, None, 'tensor'), may hold values from -0.1875 to 0.1875
- self_bias: bfloat16 [2, 1024], P(None, 'tensor'), may hold values from -3 to 3
- self_out: bfloat16 [1024, 1024], P('tensor'), may hold values from -3 to 3
- cross_qkv: bfloat16 [3, 1024, 1024], P(None, None, 'tensor'), may hold values from -0.1875 to 0.1875
- cross_bias: bfloat16 [2, 1024], P(None, 'tensor'), may hold values from -3 to 3
- cross_out: bfloat16 [1024, 1024], P('tensor'), may hold values from -3 to 3
- ffn_in: bfloat16 [1024, 4096], P(None, 'tensor'), may hold values from -0.1875 to 0.1875
- ffn_in_bias: bfloat16 [4096], P('tensor'), may hold values from -3 to 3
- ffn_out: bfloat16 [4096, 1024], P('tensor'), may hold values from -0.09375 to 0.09375
- norm_gain: bfloat16 [1024, 3], replicated, may hold values from 0.5 to 1.5
- norm_shift: bfloat16 [1024, 3], replicated, may hold values from -2 to 2
- out_bias: bfloat16 [1024, 3], replicated, may hold values from -2 to 2
- cotangent: bfloat16 [8192, 1024], P(('dp', 'tensor')), may hold values from -6 to 6
Outputs:
- output: bfloat16 [8192, 1024], P(('dp', 'tensor'))
- input_grad: bfloat16 [8192, 1024], P(('dp', 'tensor'))
- memory_grad: bfloat16 [8192, 1024], P(('dp', 'tensor'))
- self_qkv_grad: float32 [3, 1024, 1024], P(None, None, 'tensor')
- self_bias_grad: float32 [2, 1024], P(None, 'tensor')
- self_out_grad: float32 [1024, 1024], P('tensor')
- cross_qkv_grad: float32 [3, 1024, 1024], P(None, None, 'tensor')
- cross_bias_grad: float32 [2, 1024], P(None, 'tensor')
- cross_out_grad: float32 [1024, 1024], P('tensor')
- ffn_in_grad: float32 [1024, 4096], P(None, 'tensor')
- ffn_in_bias_grad: float32 [4096], P('tensor')
- ffn_out_grad: float32 [4096, 1024], P('tensor')
- norm_gain_grad: float32 [1024, 3], P('tensor')
- norm_shift_grad: float32 [1024, 3], P('tensor')
- out_bias_grad: float32 [1024, 3], P('tensor')
The draws below stay inside these ranges and needn't reach their ends.
Inputs may be any that keep to these rules, and one draw needn't show every extreme that they name: prefix[s] is the number of leading positions of sequence s whose tokens see each other both ways; some sequence has exactly 102 and some exactly 512.
All inputs are finite; a program needn't handle non-finite values.
Results may differ from the reference program's by a relative error of at most 0.024.
The reference program's roundings to bfloat16 on the way count: a program that leaves them out, or rounds other values in their place, can miss the bound.
Values may be sent and summed in bfloat16 or wider, within the bound.
A program may use at most 192 MiB of HBM per device.

```python
import math
import jax
import jax.numpy as jnp
from jax import lax

D = 1024
HEADS = 16
HEAD_DIM = 64
FF = 4096
LEN = 1024
MEM = 1024
SEQS = 8


def draw_prefix(key, part):
    first_key = jax.random.fold_in(key, 11)
    second_key = jax.random.fold_in(key, 12)
    lengths = jax.random.randint(first_key, (SEQS,), LEN // 10, LEN // 2 + 1).astype(jnp.int32)
    order = jax.random.permutation(second_key, SEQS)
    places = jnp.arange(SEQS)
    lengths = jnp.where(places == order[0], LEN // 2, lengths)
    lengths = jnp.where(places == order[1], LEN // 10, lengths)
    return lengths.astype(jnp.int32)


def block_scale(own_key, extent, pieces, least, largest):
    def one(position, blocks):
        steps = jax.random.uniform(jax.random.fold_in(jax.random.fold_in(own_key, 6), position), (blocks,), jnp.float32, least / len(pieces), largest / len(pieces))
        return jnp.repeat(jnp.exp(steps), extent[position] // blocks).reshape((-1,) + (1,) * (len(extent) - position - 1))

    factor_of = one(*pieces[0])
    for cut in pieces[1:]:
        factor_of = factor_of * one(*cut)
    return factor_of


def normal_values(stream_key, dims, width, reach, pieces=(), held_as=jnp.bfloat16):
    array = width * jax.random.normal(stream_key, dims, jnp.float32)
    if pieces:
        array = array * block_scale(stream_key, dims, pieces, -0.22, 0.18)
    return jnp.clip(array, -reach, reach).astype(held_as)


def setup_inputs(seed: int = 0) -> dict:
    arg_keys = jax.random.split(jax.random.key(seed), 17)
    inputs = normal_values(arg_keys[0], (SEQS * LEN, D), 1.0, 6.0, ((0, 8),))
    memory = normal_values(arg_keys[1], (SEQS * MEM, D), 1.0, 6.0, ((0, 8),))
    prefix = draw_prefix(jax.random.fold_in(arg_keys[16], 71), 0)
    self_qkv = normal_values(arg_keys[3], (3, D, D), D ** -0.5, 0.1875, ((2, 4),))
    self_bias = normal_values(arg_keys[4], (2, D), 0.5, 3.0, ((1, 4),))
    self_out = normal_values(arg_keys[5], (D, D), (max(1, 4 * D // LEN)) ** -0.5, 3.0, ((0, 4),))
    cross_qkv = normal_values(arg_keys[6], (3, D, D), D ** -0.5, 0.1875, ((2, 4),))
    cross_bias = normal_values(arg_keys[7], (2, D), 0.5, 3.0, ((1, 4),))
    cross_out = normal_values(arg_keys[8], (D, D), (max(1, 4 * D // MEM)) ** -0.5, 3.0, ((0, 4),))
    ffn_in = normal_values(arg_keys[9], (D, FF), D ** -0.5, 0.1875, ((1, 4),))
    ffn_in_bias = normal_values(arg_keys[10], (FF,), 0.5, 3.0, ((0, 4),))
    ffn_out = normal_values(arg_keys[11], (FF, D), FF ** -0.5, 0.09375, ((0, 4),))
    norm_gain = jnp.clip(1.0 + 0.1 * jax.random.normal(arg_keys[12], (D, 3), jnp.float32), 0.5, 1.5).astype(jnp.bfloat16)
    norm_shift = normal_values(arg_keys[13], (D, 3), 0.3, 2.0)
    out_bias = normal_values(arg_keys[14], (D, 3), 0.3, 2.0)
    cotangent = normal_values(arg_keys[15], (SEQS * LEN, D), 1.0, 6.0, ((0, 32),))
    return {"inputs": inputs, "memory": memory, "prefix": prefix, "self_qkv": self_qkv, "self_bias": self_bias, "self_out": self_out, "cross_qkv": cross_qkv, "cross_bias": cross_bias, "cross_out": cross_out, "ffn_in": ffn_in, "ffn_in_bias": ffn_in_bias, "ffn_out": ffn_out, "norm_gain": norm_gain, "norm_shift": norm_shift, "out_bias": out_bias, "cotangent": cotangent}


@jax.custom_vjp
def low(v):
    return lax.optimization_barrier(v.astype(jnp.bfloat16)).astype(jnp.float32)

@jax.custom_vjp
def low_back(v):
    return v

def low_keep(v):
    return (low(v), None)

def low_pass(kept, grad):
    return (grad,)

def back_keep(v):
    return (v, None)

def back_low(kept, grad):
    return (low(grad),)
low.defvjp(low_keep, low_pass)
low_back.defvjp(back_keep, back_low)
epsilon = 1e-05
masked_score = -1e+30

def layer_norm(values, gains, shifts):
    centered = values - lax.optimization_barrier(jnp.mean(values, axis=-1, keepdims=True))
    variance = lax.optimization_barrier(jnp.mean(centered * centered, axis=-1, keepdims=True))
    return centered * lax.rsqrt(variance + epsilon) * gains + shifts

def matmul(lhs_rows, weight):
    return jnp.dot(lhs_rows, weight, precision=lax.Precision.HIGHEST)

def gelu_exact(values):
    return 0.5 * values * (1.0 + lax.erf(values * (1.0 / math.sqrt(2.0))))

def attention(queries, key_rows, values, allowed):
    query_heads = queries.reshape(queries.shape[0], HEADS, HEAD_DIM)
    key_heads = key_rows.reshape(key_rows.shape[0], HEADS, HEAD_DIM)
    value_heads = values.reshape(values.shape[0], HEADS, HEAD_DIM)
    scores = jnp.einsum('lhe,mhe->hlm', query_heads, key_heads, precision=lax.Precision.HIGHEST) * (1.0 / math.sqrt(HEAD_DIM))
    scores = low_back(scores)
    scores = jnp.where(allowed[None], scores, masked_score)
    highest = lax.optimization_barrier(jnp.max(scores, axis=-1, keepdims=True))
    weights = jnp.exp(scores - highest)
    probability = low(weights / lax.optimization_barrier(jnp.sum(weights, axis=-1, keepdims=True)))
    context = jnp.einsum('hlm,mhe->lhe', probability, value_heads, precision=lax.Precision.HIGHEST)
    return low(low_back(context.reshape(queries.shape[0], HEADS * HEAD_DIM)))

def sequence_layer(params, tokens, memory_rows, limit):
    self_qkv, self_bias, self_out, cross_qkv, cross_bias, cross_out, ffn_in, ffn_in_bias, ffn_out, norm_gain, norm_shift, out_bias = params
    places = jnp.arange(LEN)
    allowed = (places[None, :] <= places[:, None]) | (places[None, :] < limit)
    self_query = low(low_back(matmul(tokens, self_qkv[0])) + self_bias[0])
    self_key = low(low_back(matmul(tokens, self_qkv[1])))
    self_value = low(low_back(matmul(tokens, self_qkv[2])) + self_bias[1])
    self_context = attention(self_query, self_key, self_value, allowed)
    middle = layer_norm(tokens + low_back(matmul(self_context, self_out)) + out_bias[:, 0], norm_gain[:, 0], norm_shift[:, 0])
    middle_low = low(middle)
    cross_query = low(low_back(matmul(middle_low, cross_qkv[0])) + cross_bias[0])
    cross_key = low(low_back(matmul(memory_rows, cross_qkv[1])))
    cross_value = low(low_back(matmul(memory_rows, cross_qkv[2])) + cross_bias[1])
    every_key = jnp.ones((LEN, MEM), dtype=bool)
    cross_context = attention(cross_query, cross_key, cross_value, every_key)
    second = layer_norm(middle + low_back(matmul(cross_context, cross_out)) + out_bias[:, 1], norm_gain[:, 1], norm_shift[:, 1])
    second_low = low(second)
    hidden_pre = low_back(matmul(second_low, ffn_in)) + ffn_in_bias
    hidden_act = low(gelu_exact(hidden_pre))
    return layer_norm(second + low_back(matmul(hidden_act, ffn_out)) + out_bias[:, 2], norm_gain[:, 2], norm_shift[:, 2])

def forward(params, tokens, memory_rows, prefix):
    token_seqs = tokens.reshape(SEQS, LEN, D)
    memory_seqs = memory_rows.reshape(SEQS, MEM, D)
    layer = jax.checkpoint(sequence_layer)

    def advance(carry, packed):
        return (carry, layer(params, packed[0], packed[1], packed[2]))
    _, results = lax.scan(advance, jnp.zeros((), jnp.float32), (token_seqs, memory_seqs, prefix))
    return results.reshape(SEQS * LEN, D)

def reference(inputs, memory, prefix, self_qkv, self_bias, self_out, cross_qkv, cross_bias, cross_out, ffn_in, ffn_in_bias, ffn_out, norm_gain, norm_shift, out_bias, cotangent):
    params = tuple((weight.astype(jnp.float32) for weight in (self_qkv, self_bias, self_out, cross_qkv, cross_bias, cross_out, ffn_in, ffn_in_bias, ffn_out, norm_gain, norm_shift, out_bias)))
    tokens = inputs.astype(jnp.float32)
    memory_rows = memory.astype(jnp.float32)

    def run(weights, token_rows, memory_part):
        return forward(weights, token_rows, memory_part, prefix)
    result, pullback = jax.vjp(run, params, tokens, memory_rows)
    grads, input_grad, memory_grad = pullback(cotangent.astype(jnp.float32))
    return (result.astype(jnp.bfloat16), input_grad.astype(jnp.bfloat16), memory_grad.astype(jnp.bfloat16), grads[0], grads[1], grads[2], grads[3], grads[4], grads[5], grads[6], grads[7], grads[8], grads[9], grads[10], grads[11])
```

```python
import functools
import math

import jax
import jax.numpy as jnp
from jax import lax
from jax.experimental import pallas as pl
from jax.experimental.pallas import tpu as pltpu
from jax.sharding import PartitionSpec as P

HEAD_DIM = 64
EPS = 1e-05
MASKED = -1e30
F32 = jnp.float32
BF16 = jnp.bfloat16
MESH = pl.DeviceIdType.MESH
ANY = pl.BlockSpec(memory_space=pl.ANY)
VMEM = pl.BlockSpec(memory_space=pltpu.VMEM)
SMEM = pl.BlockSpec(memory_space=pltpu.SMEM)
NN = (((1,), (0,)), ((), ()))
NT = (((1,), (1,)), ((), ()))
TN = (((0,), (0,)), ((), ()))


def mm(a, b, dims=NN):
    return lax.dot_general(a, b, dims, preferred_element_type=F32)


def fold(v):
    return jnp.sum(v.reshape(-1, 8, v.shape[-1]), axis=0)


def layer_kernel(
    T, D, HC, FF,
    x_hbm, mem_hbm, prefix_ref, wsq_hbm, wso_hbm, wcq_hbm, wco_hbm, w1_hbm, w2_hbm, cot_hbm,
    norm_ref, sbias_ref, cbias_ref, fbias_ref,
    out_hbm, ig_hbm, mg_hbm, gsq_hbm, gso_hbm, gcq_hbm, gco_hbm, g1_hbm, g2_hbm, small_ref,
    xin, mem, wsq, wso, wcq, wco, w1, w2, cot,
    q1, k1, v1, c1, q2, k2, v2, c2, lse1, lse2,
    mlow, slow, d3l, d2l, act, slope, dpre,
    n1, n2, inv1, inv2, dcur,
    chip_send, chip_recv, acc, x_send, x_recv,
    dql, dkl, dvl, kT, dqT, qm, dom, up, G,
    sums, fsum, hsum,
    in_sems, out_sems, cs_sem, cr_sem, xs_sem, xr_sem, as_sem, ar_sem,
):
    H = HC // HEAD_DIM
    obuf = cot
    units = [(G, u * (T // 4)) for u in range(8)] + [(slow, u * (T // 4)) for u in range(4)] + [
        (w1, u * (T // 4)) for u in range(4)]
    CH = T // 2
    R = T // 4
    dp = lax.axis_index("dp")
    tn = lax.axis_index("tensor")
    xi = tn // 2
    ci = lax.rem(tn, 2)
    mate = (dp, xi * 2 + (1 - ci))
    peer = (dp, (1 - xi) * 2 + ci)

    srcs = [(x_hbm, xin), (wsq_hbm, wsq), (wso_hbm, wso), (mem_hbm, mem), (wcq_hbm, wcq), (wco_hbm, wco),
            (w1_hbm, w1), (w2_hbm, w2)]
    loads = [pltpu.make_async_copy(a, b, in_sems.at[i]) for i, (a, b) in enumerate(srcs)]
    loads.append(pltpu.make_async_copy(cot_hbm, cot.at[xi], in_sems.at[len(srcs)]))
    for load in loads:
        load.start()
    XIN, WSQ, WSO, MEMR, WCQ, WCO, W1, W2, COT = range(9)

    barrier = pltpu.get_barrier_semaphore()
    for other in (mate, peer):
        pl.semaphore_signal(barrier, inc=1, device_id=other, device_id_type=MESH)
    pl.semaphore_wait(barrier, 2)

    loads[COT].wait()
    cot_copy = pltpu.make_async_remote_copy(
        src_ref=cot.at[xi], dst_ref=cot.at[xi], send_sem=xs_sem.at[0, 0], recv_sem=xr_sem.at[0, 0],
        device_id=peer, device_id_type=MESH)
    cot_copy.start()

    sums[...] = jnp.zeros_like(sums)
    fsum[...] = jnp.zeros_like(fsum)
    hsum[...] = jnp.zeros_like(hsum)

    def mine(j):
        return pl.multiple_of(j * CH + ci * R, R)

    def mates(j):
        return pl.multiple_of(j * CH + (1 - ci) * R, R)

    def head_mask(h):
        lane = lax.broadcasted_iota(jnp.int32, (8, HC), 1)
        return jnp.where(lane // HEAD_DIM == h, 1.0, 0.0)[0:1].astype(BF16)

    def project(src, w, wi, bias, dst, r0, n, scale=None):
        @pl.loop(0, n // R)
        def _(i):
            r = pl.multiple_of(r0 + i * R, R)
            y = mm(src[pl.ds(r, R), :], w[wi])
            if bias is not None:
                y = y + bias
            y = y.astype(BF16)
            if scale is not None:
                y = y * jnp.asarray(scale, BF16)
            dst[pl.ds(r, R), :] = y

    SC = 1.0 / math.sqrt(HEAD_DIM)

    def visible(keys_first, r0, nk):
        if keys_first:
            shape, kd = (nk, R), 0
        else:
            shape, kd = (R, nk), 1
        key = lax.broadcasted_iota(jnp.int32, shape, kd)
        row = lax.broadcasted_iota(jnp.int32, shape, 1 - kd) + r0
        return (key <= row) | (key < prefix_ref[0])

    def attend(q, k, v, c, lse, j, causal):
        for i in range(CH // R):
            r0 = j * CH + i * R
            nk = max(T // 2, r0 + R) if causal else T
            rows = slice(r0, r0 + R)
            lane = lax.broadcasted_iota(jnp.int32, (R, 128), 1)
            for h in range(H):
                m = head_mask(h)
                s = mm(q[rows, :] * m, k[:nk, :], NT)
                if causal:
                    s = jnp.where(visible(False, r0, nk), s, MASKED)
                top = jnp.max(s, axis=1, keepdims=True)
                e = jnp.exp(s - top)
                tot = jnp.sum(e, axis=1, keepdims=True)
                p = (e * (1.0 / tot)).astype(BF16)
                o = mm(p, v[:nk, :] * m)
                l = top + jnp.log(tot)
                if h == 0:
                    dqT[...] = o
                    stat = jnp.where(lane == h, l, 0.0)
                else:
                    dqT[...] += o
                    stat = jnp.where(lane == h, l, stat)
            c[rows, :] = dqT[...].astype(BF16)
            lse[:, rows] = jnp.transpose(stat)[0:8, :]

    def attend_back(q, k, v, lse, j, causal, dk, dv, first, slot):
        pbuf, sbuf = act, dpre
        for i in range(CH // R):
            r0 = j * CH + i * R
            nk = max(T // 2, r0 + R) if causal else T
            rows = slice(r0, r0 + R)

            @pl.loop(0, H)
            def _(h):
                m = head_mask(h)
                qh = q[rows, :] * m
                doh = up[i * R:(i + 1) * R, :] * m
                cols = pl.ds(pl.multiple_of(h * R, R), R)
                qm[cols, :] = qh
                dom[cols, :] = doh
                s = mm(k[:nk, :], qh, NT)
                if causal:
                    s = jnp.where(visible(True, r0, nk), s, MASKED)
                p = jnp.exp(s - lse[pl.ds(h, 1), rows])
                dpv = mm(v[:nk, :], doh, NT)
                dd = jnp.sum(p * dpv, axis=0, keepdims=True)
                ds = (p * (dpv - dd)).astype(BF16)
                pbuf[:nk, cols] = p.astype(BF16)
                sbuf[:nk, cols] = ds
                hr = pl.ds(pl.multiple_of(h * HEAD_DIM, HEAD_DIM), HEAD_DIM)
                dqT[hr, :] = mm(kT[hr, :nk], ds)

            @pl.loop(0, nk // R)
            def _(kt):
                kr = pl.ds(pl.multiple_of(kt * R, R), R)
                a = mm(pbuf[kr, :], dom[...])
                b = mm(sbuf[kr, :], qm[...])
                if first and i == 0:
                    dv[kr, :] = a
                    dk[kr, :] = b
                else:
                    dv[kr, :] += a
                    dk[kr, :] += b

            if first and i == 0 and nk < T:
                dv[nk:, :] = jnp.zeros((T - nk, HC), F32)
                dk[nk:, :] = jnp.zeros((T - nk, HC), F32)
            dq = jnp.transpose(dqT[...]) * SC
            hsum[slot] += fold(dq)
            dql[rows, :] = dq.astype(BF16)

    def finish_back(dk, dv, slot):
        @pl.loop(0, T // R)
        def _(i):
            r = pl.ds(pl.multiple_of(i * R, R), R)
            a = dv[r, :]
            hsum[slot + 1] += fold(a)
            dvl[r, :] = a.astype(BF16)
            dkl[r, :] = dk[r, :].astype(BF16)

    def chip_copy(s, j):
        dst = mlow.at[pl.ds(j * R, R)] if s == 7 else chip_recv.at[j]
        return pltpu.make_async_remote_copy(
            src_ref=chip_send.at[j], dst_ref=dst, send_sem=cs_sem.at[s, j], recv_sem=cr_sem.at[s, j],
            device_id=mate, device_id_type=MESH)

    def x_copy(s, j):
        return pltpu.make_async_remote_copy(
            src_ref=x_send.at[j], dst_ref=x_recv.at[s % 2, j], send_sem=xs_sem.at[s, j], recv_sem=xr_sem.at[s, j],
            device_id=peer, device_id_type=MESH)

    def low_copy(s, j, low):
        rows = pl.ds(mine(j), R)
        return pltpu.make_async_remote_copy(
            src_ref=low.at[rows], dst_ref=low.at[rows], send_sem=as_sem.at[s, j], recv_sem=ar_sem.at[s, j],
            device_id=mate, device_id_type=MESH)

    NTILE = 256

    def partial(s, j, terms):
        def tile(r, n):
            y = None
            for lhs, rhs, dims in terms:
                t = mm(lhs[pl.ds(r, R), :], rhs(n), dims)
                y = t if y is None else y + t
            return y

        @pl.loop(0, D // NTILE)
        def _(n):
            n = pl.ds(pl.multiple_of(n * NTILE, NTILE), NTILE)
            chip_send[j, :, n] = tile(mates(j), n).astype(BF16)

        chip_copy(s, j).start()

        @pl.loop(0, D // NTILE)
        def _(n):
            n = pl.ds(pl.multiple_of(n * NTILE, NTILE), NTILE)
            acc[j, :, n] = tile(mine(j), n)

    RT = 32

    def chip_sum(s, j):
        chip_copy(s, j).wait()

        @pl.loop(0, R // RT)
        def _(i):
            r = pl.ds(pl.multiple_of(i * RT, RT), RT)
            x_send[j, r, :] = (acc[j, r, :] + chip_recv[j, r, :].astype(F32)).astype(BF16)

        x_copy(s, j).start()

    def total(s, j, r):
        return x_send[j, r, :].astype(F32) + x_recv[s % 2, j, r, :].astype(F32)

    def gain(i):
        return norm_ref[i:i + 1, :]

    def shift(i):
        return norm_ref[3 + i:4 + i, :]

    def obias(i):
        return norm_ref[6 + i:7 + i, :]

    def normed(v):
        cen = v - jnp.mean(v, axis=-1, keepdims=True)
        inv = lax.rsqrt(jnp.mean(cen * cen, axis=-1, keepdims=True) + EPS)
        return cen * inv, inv

    def norm_back(dy, n, inv, i):
        g = dy * gain(i)
        dv = inv * (g - jnp.mean(g, axis=-1, keepdims=True) - n * jnp.mean(g * n, axis=-1, keepdims=True))
        sums[i] += fold(dy * n)
        sums[3 + i] += fold(dy)
        sums[6 + i] += fold(dv)
        return dv

    def finish(s, j, low):
        x_copy(s, j).wait()
        base = mine(j)

        @pl.loop(0, R // RT)
        def _(i):
            r = pl.ds(pl.multiple_of(i * RT, RT), RT)
            g = pl.ds(pl.multiple_of(base + i * RT, RT), RT)
            t = total(s, j, r)
            if s == 1:
                n, inv = normed(xin[g, :].astype(F32) + t + obias(0))
                n1[j, r, :] = n
                inv1[j, r, :] = jnp.broadcast_to(inv, (RT, 128))
                low[g, :] = (n * gain(0) + shift(0)).astype(BF16)
            elif s == 2:
                n, inv = normed(n1[j, r, :] * gain(0) + shift(0) + t + obias(1))
                n2[j, r, :] = n
                inv2[j, r, :] = jnp.broadcast_to(inv, (RT, 128))
                low[g, :] = (n * gain(1) + shift(1)).astype(BF16)
            elif s == 3:
                n, inv = normed(n2[j, r, :] * gain(1) + shift(1) + t + obias(2))
                dy = cot[j, r, :].astype(F32)
                obuf[j, r, :] = (n * gain(2) + shift(2)).astype(BF16)
                d = norm_back(dy, n, inv, 2)
                dcur[j, r, :] = d
                low[g, :] = d.astype(BF16)
            elif s == 4:
                d = norm_back(dcur[j, r, :] + t, n2[j, r, :], inv2[j, r, 0:1], 1)
                dcur[j, r, :] = d
                low[g, :] = d.astype(BF16)
            else:
                d = norm_back(dcur[j, r, :] + t, n1[j, r, :], inv1[j, r, 0:1], 0)
                dcur[j, r, :] = d
                low[g, :] = d.astype(BF16)

        low_copy(s, j, low).start()

    def gather(s, j, low):
        low_copy(s, j, low).wait()

    def got(s, j, i):
        if s == 7:
            return mlow[pl.ds(pl.multiple_of(j * R + i * RT, RT), RT), :].astype(F32)
        return chip_recv[j, pl.ds(pl.multiple_of(i * RT, RT), RT), :].astype(F32)

    def scatter_send(s):
        for j in range(2):
            chip_copy(s, j).wait()
        j = 1 - xi

        @pl.loop(0, R // RT)
        def _(i):
            r = pl.ds(pl.multiple_of(i * RT, RT), RT)
            x_send[0, r, :] = (acc[j, r, :] + got(s, j, i)).astype(BF16)

        x_copy(s, 0).start()

    def scatter_finish(s, extra, dst):
        x_copy(s, 0).wait()

        @pl.loop(0, R // RT)
        def _(i):
            r = pl.ds(pl.multiple_of(i * RT, RT), RT)
            t = acc[xi, r, :] + got(s, xi, i) + x_recv[s % 2, 0, r, :].astype(F32)
            if extra is not None:
                t = t + extra[xi, r, :]
            dst[r, :] = t.astype(BF16)

    def grad_rows(u, lhs, c0, rhs):
        @pl.loop(0, D // NTILE)
        def _(n):
            n = pl.ds(pl.multiple_of(n * NTILE, NTILE), NTILE)
            unit, r0 = units[u]
            unit[r0:r0 + R, n] = mm(lhs[:, pl.ds(c0, R)], rhs[:, n], TN).astype(BF16)

    def grad_cols(pairs, lhs):
        @pl.loop(0, D // R)
        def _(b):
            cols = pl.ds(pl.multiple_of(b * R, R), R)
            for u, rhs in pairs:
                unit, r0 = units[u]
                unit[r0:r0 + R, cols] = mm(lhs[:, cols], rhs[...], TN).astype(BF16)

    loads[XIN].wait()
    loads[WSQ].wait()
    project(xin, wsq, 0, sbias_ref[0:1, :], q1, 0, T, SC)
    project(xin, wsq, 1, None, k1, 0, T)
    project(xin, wsq, 2, sbias_ref[1:2, :], v1, 0, T)
    loads[WSO].wait()

    def self_forward(j):
        attend(q1, k1, v1, c1, lse1, j, True)
        partial(1, j, [(c1, lambda n: wso[:, n], NN)])
        chip_sum(1, j)

    def cross_forward(j):
        project(mlow, wcq, 0, cbias_ref[0:1, :], q2, j * CH, CH, SC)
        attend(q2, k2, v2, c2, lse2, j, False)
        partial(2, j, [(c2, lambda n: wco[:, n], NN)])
        chip_sum(2, j)

    def ffn_forward(j):
        @pl.loop(0, CH // R)
        def _(i):
            r = pl.ds(pl.multiple_of(j * CH + i * R, R), R)

            @pl.loop(0, FF // NTILE)
            def _(n):
                cols = pl.ds(pl.multiple_of(n * NTILE, NTILE), NTILE)
                pre = mm(slow[r, :], w1[:, cols]) + fbias_ref[:, cols]
                half = 0.5 * (1.0 + lax.erf(pre * (1.0 / math.sqrt(2.0))))
                act[r, cols] = (pre * half).astype(BF16)
                slope[n, r, :] = half + pre * jnp.exp(-0.5 * pre * pre) * (1.0 / math.sqrt(2.0 * math.pi))

        partial(3, j, [(act, lambda n: w2[:, n], NN)])
        chip_sum(3, j)

    def ffn_backward(j):
        @pl.loop(0, CH // R)
        def _(i):
            r = pl.ds(pl.multiple_of(j * CH + i * R, R), R)

            @pl.loop(0, FF // NTILE)
            def _(n):
                cols = pl.ds(pl.multiple_of(n * NTILE, NTILE), NTILE)
                t = mm(d3l[r, :], w2[cols, :], NT) * slope[n, r, :]
                fsum[:, cols] += fold(t)
                dpre[r, cols] = t.astype(BF16)

        partial(4, j, [(dpre, lambda n: w1[n, :], NT)])
        chip_sum(4, j)

    self_forward(0)
    self_forward(1)
    loads[MEMR].wait()
    loads[WCQ].wait()
    project(mem, wcq, 1, None, k2, 0, T)
    project(mem, wcq, 2, cbias_ref[1:2, :], v2, 0, T)
    loads[WCO].wait()
    finish(1, 0, mlow)
    gather(1, 0, mlow)
    cross_forward(0)
    finish(1, 1, mlow)
    gather(1, 1, mlow)
    cross_forward(1)
    loads[W1].wait()
    loads[W2].wait()
    finish(2, 0, slow)
    gather(2, 0, slow)
    ffn_forward(0)
    finish(2, 1, slow)
    gather(2, 1, slow)
    ffn_forward(1)
    cot_copy.wait()
    finish(3, 0, d3l)
    gather(3, 0, d3l)
    ffn_backward(0)
    finish(3, 1, d3l)
    gather(3, 1, d3l)
    ffn_backward(1)
    out_copy = pltpu.make_async_copy(obuf.at[xi], out_hbm, out_sems.at[0])
    out_copy.start()
    for u in range(4):
        grad_rows(u, act, u * R, d3l)
    for u in range(4):
        grad_rows(4 + u, slow, u * R, dpre)
    out_copies = [out_copy]

    def emit(i, src, dst):
        if isinstance(src, tuple):
            u, cols = src
            src = units[u][0].at[pl.ds(units[u][1], R)]
            if cols != slice(None):
                src = units[u][0].at[pl.ds(units[u][1], R), cols]
        c = pltpu.make_async_copy(src, dst, out_sems.at[i])
        c.start()
        out_copies.append(c)

    for u in range(4):
        emit(1 + u, (u, slice(None)), g2_hbm.at[pl.ds(u * R, R)])
        emit(5 + u, (4 + u, slice(None)), g1_hbm.at[pl.ds(u * R, R)])

    def upstream(low, wo, j):
        @pl.loop(0, CH // R)
        def _(i):
            r = pl.ds(pl.multiple_of(j * CH + i * R, R), R)
            up[pl.ds(pl.multiple_of(i * R, R), R), :] = mm(low[r, :], wo[...], NT).astype(BF16)

    dk, dv = slope.at[0], slope.at[1]

    def cross_backward(j):
        upstream(d2l, wco, j)
        attend_back(q2, k2, v2, lse2, j, False, dk, dv, j == 0, 2)
        partial(5, j, [(dql, lambda n: wcq[0, n, :], NT)])
        chip_sum(5, j)

    kT[...] = jnp.transpose(k2[...])
    finish(4, 0, d2l)
    gather(4, 0, d2l)
    cross_backward(0)
    finish(4, 1, d2l)
    gather(4, 1, d2l)
    cross_backward(1)
    finish_back(dk, dv, 2)
    grad_rows(8, c2, 0, d2l)
    grad_cols([(9, dql)], mlow)
    grad_cols([(10, dkl), (11, dvl)], mem)
    emit(9, (8, slice(None)), gco_hbm)
    for u in range(3):
        for b in range(D // R):
            emit(10 + 4 * u + b, (9 + u, pl.ds(b * R, R)), gcq_hbm.at[u, pl.ds(b * R, R)])

    kT[...] = jnp.transpose(k1[...])
    d1l = d3l
    finish(5, 0, d1l)
    finish(5, 1, d1l)
    gather(5, 0, d1l)
    gather(5, 1, d1l)
    for j in range(2):
        partial(6, j, [(dkl, lambda n: wcq[1, n, :], NT), (dvl, lambda n: wcq[2, n, :], NT)])
    scatter_send(6)
    for j in range(2):
        upstream(d1l, wso, j)
        attend_back(q1, k1, v1, lse1, j, True, dk, dv, j == 0, 0)
    scatter_finish(6, None, mem_out := obuf.at[1 - xi])
    emit(22, mem_out, mg_hbm)
    finish_back(dk, dv, 0)
    for j in range(2):
        partial(7, j, [(dql, lambda n: wsq[0, n, :], NT), (dkl, lambda n: wsq[1, n, :], NT),
                       (dvl, lambda n: wsq[2, n, :], NT)])
    scatter_send(7)
    grad_rows(12, c1, 0, d1l)
    grad_cols([(13, dql), (14, dkl), (15, dvl)], xin)
    emit(23, (12, slice(None)), gso_hbm)
    for u in range(3):
        for b in range(D // R):
            emit(24 + 4 * u + b, (13 + u, pl.ds(b * R, R)), gsq_hbm.at[u, pl.ds(b * R, R)])
    out_copy.wait()
    scatter_finish(7, dcur, obuf.at[xi])
    emit(36, obuf.at[xi], ig_hbm)
    small_ref[...] = jnp.zeros_like(small_ref)
    for i in range(9):
        small_ref[i:i + 1, :] = jnp.sum(sums[i], axis=0, keepdims=True)
    small_ref[9:10, :] = jnp.sum(fsum[...], axis=0, keepdims=True)
    for i in range(4):
        small_ref[10:11, i * HC:(i + 1) * HC] = jnp.sum(hsum[i], axis=0, keepdims=True)
    for c in out_copies[1:]:
        c.wait()


def shards(inputs, memory, prefix, self_qkv, self_bias, self_out, cross_qkv, cross_bias, cross_out,
           ffn_in, ffn_in_bias, ffn_out, norm_gain, norm_shift, out_bias, cotangent):
    T, D = inputs.shape
    HC = self_out.shape[0]
    FF = ffn_out.shape[0]
    R = T // 4
    norms = jnp.concatenate(
        [norm_gain.T, norm_shift.T, out_bias.T, jnp.zeros((7, D), BF16)], axis=0).astype(F32)
    sds = jax.ShapeDtypeStruct
    v = pltpu.VMEM
    dma = pltpu.SemaphoreType.DMA
    outs = pl.pallas_call(
        functools.partial(layer_kernel, T, D, HC, FF),
        out_shape=(
            sds((R, D), BF16), sds((R, D), BF16), sds((R, D), BF16),
            sds((3, D, HC), BF16), sds((HC, D), BF16), sds((3, D, HC), BF16), sds((HC, D), BF16),
            sds((D, FF), BF16), sds((FF, D), BF16), sds((16, D), F32),
        ),
        in_specs=[ANY, ANY, SMEM] + [ANY] * 7 + [VMEM] * 4,
        out_specs=(ANY,) * 9 + (VMEM,),
        scratch_shapes=[
            v((T, D), BF16), v((T, D), BF16), v((3, D, HC), BF16), v((HC, D), BF16), v((3, D, HC), BF16),
            v((HC, D), BF16), v((D, FF), BF16), v((FF, D), BF16), v((2, R, D), BF16),
        ] + [v((T, HC), BF16)] * 8 + [v((8, T), F32)] * 2 + [
            v((T, D), BF16), v((T, D), BF16), v((T, D), BF16), v((T, D), BF16),
            v((T, FF), BF16), v((FF // 256, T, 256), F32), v((T, FF), BF16),
            v((2, R, D), F32), v((2, R, D), F32), v((2, R, 128), F32), v((2, R, 128), F32), v((2, R, D), F32),
            v((2, R, D), BF16), v((2, R, D), BF16), v((2, R, D), F32), v((2, R, D), BF16), v((2, 2, R, D), BF16),
            v((T, HC), BF16), v((T, HC), BF16), v((T, HC), BF16), v((HC, T), BF16), v((HC, R), F32),
            v((4 * R, HC), BF16), v((4 * R, HC), BF16), v((T // 2, HC), BF16), v((8 * R, D), BF16),
            v((9, 8, D), F32), v((8, FF), F32), v((4, 8, HC), F32),
            dma((9,)), dma((40,)), dma((8, 2)), dma((8, 2)), dma((8, 2)), dma((8, 2)), dma((8, 2)), dma((8, 2)),
        ],
        compiler_params=pltpu.CompilerParams(
            collective_id=0, has_side_effects=True, vmem_limit_bytes=64 * 2**20 - 256 * 1024),
    )(inputs, memory, prefix, self_qkv, self_out, cross_qkv, cross_out, ffn_in, ffn_out, cotangent,
      norms, self_bias.astype(F32), cross_bias.astype(F32), ffn_in_bias.astype(F32)[None, :])
    out, ig, mg, gsq, gso, gcq, gco, g1, g2, small = outs
    summed = lax.psum((gsq, gso, gcq, gco, g1, g2), "dp")
    gsq, gso, gcq, gco, g1, g2 = [a.astype(F32) for a in summed]
    norm_rows = lax.psum(small[:9], ("dp", "tensor")) * 0.5
    rest = lax.psum(small[9:11], "dp")
    share = D // lax.axis_size("tensor")
    norm_rows = lax.dynamic_slice_in_dim(norm_rows, lax.axis_index("tensor") * share, share, 1).T
    hb = rest[1].reshape(4, HC)
    return (out, ig, mg, gsq, hb[0:2], gso, gcq, hb[2:4], gco, g1, rest[0], g2,
            norm_rows[:, 0:3], norm_rows[:, 3:6], norm_rows[:, 6:9])


def solution(mesh):
    t = "tensor"
    return jax.shard_map(
        shards,
        mesh=mesh,
        in_specs=(
            P("dp", None), P("dp", None), P("dp"), P(None, None, t), P(None, t), P(t, None), P(None, None, t),
            P(None, t), P(t, None), P(None, t), P(t), P(t, None), P(), P(), P(), P(("dp", t), None),
        ),
        out_specs=(
            P(("dp", t), None), P(("dp", t), None), P(("dp", t), None), P(None, None, t), P(None, t), P(t, None),
            P(None, None, t), P(None, t), P(t, None), P(None, t), P(t), P(t, None), P(t, None), P(t, None),
            P(t, None),
        ),
        check_vma=False,
    )
```

```python
import functools
import math

import jax
import jax.numpy as jnp
from jax import lax
from jax.experimental import pallas as pl
from jax.experimental.pallas import tpu as pltpu
from jax.sharding import PartitionSpec as P

HEAD_DIM = 64
EPS = 1e-05
MASKED = -1e30
SLOTS = 8
LAG = (1, 2, 2, 1, 2, 2, 1)
LAST = (1, 1, 1, 1, 1, 1, 1)
F32 = jnp.float32
BF16 = jnp.bfloat16
MESH = pl.DeviceIdType.MESH
ANY = pl.BlockSpec(memory_space=pl.ANY)
VMEM = pl.BlockSpec(memory_space=pltpu.VMEM)
SMEM = pl.BlockSpec(memory_space=pltpu.SMEM)
NN = (((1,), (0,)), ((), ()))
NT = (((1,), (1,)), ((), ()))
TN = (((0,), (0,)), ((), ()))


def mm(a, b, dims=NN):
    return lax.dot_general(a, b, dims, preferred_element_type=F32)


def fold(v):
    return jnp.sum(v.reshape(-1, 8, v.shape[-1]), axis=0)


def layer_kernel(
    T, D, HC, FF,
    x_hbm, mem_hbm, prefix_ref, wsq_hbm, wso_hbm, wcq_hbm, wco_hbm, w1_hbm, w2_hbm, cot_hbm,
    norm_ref, sbias_ref, cbias_ref,
    out_hbm, ig_hbm, mg_hbm, gsq_hbm, gso_hbm, gcq_hbm, gco_hbm, g1_hbm, g2_hbm, small_ref,
    xin, mem, wsq, wso, wcq, wco, w1, w2, cot,
    q1, k1, v1, c1, q2, k2, v2, c2, lse1, lse2,
    mlow, slow, d3l, d2l, act, slope, dpre,
    n1, n2, inv1, inv2, dcur,
    chip_send, chip_recv, acc, x_send, x_recv,
    dql, dkl, dvl, kT, dqT, qm, dom, up, ring, sring,
    sums, fsum, hsum,
    in_sems, out_sems, cs_sem, cr_sem, xs_sem, xr_sem, as_sem, ar_sem, ds_sem, dr_sem, do_sem, ss_sem, sr_sem,
):
    H = HC // HEAD_DIM
    obuf = cot
    units = [(ref, u * (T // 4)) for ref in (xin, w2, slow, w1) for u in range(4)]
    CH = T // 2
    R = T // 4
    dp = lax.axis_index("dp")
    tn = lax.axis_index("tensor")
    xi = tn // 2
    ci = lax.rem(tn, 2)
    mate = (dp, xi * 2 + (1 - ci))
    peer = (dp, (1 - xi) * 2 + ci)
    yi = lax.rem(dp, 2)
    zi = lax.rem(dp // 2, 4)
    inner = (zi == 1) | (zi == 2)
    outer = jnp.logical_not(inner)
    ymate = (dp + 1 - 2 * yi, tn)
    zmate = (dp + 2 - 4 * lax.rem(zi, 2), tn)
    across = (dp + 6 - 4 * zi, tn)

    srcs = [(x_hbm, xin), (wsq_hbm, wsq), (wso_hbm, wso), (mem_hbm, mem), (wcq_hbm, wcq), (wco_hbm, wco),
            (w1_hbm, w1), (w2_hbm, w2)]
    loads = [pltpu.make_async_copy(a, b, in_sems.at[i]) for i, (a, b) in enumerate(srcs)]
    loads.append(pltpu.make_async_copy(cot_hbm, cot.at[xi], in_sems.at[len(srcs)]))
    XIN, WSQ, WSO, MEMR, WCQ, WCO, W1, W2, COT = range(9)
    loads[COT].start()
    barrier = pltpu.get_barrier_semaphore()
    for other in (mate, peer, ymate, zmate):
        pl.semaphore_signal(barrier, inc=1, device_id=other, device_id_type=MESH)
    loads[COT].wait()
    for i in (XIN, WSQ):
        loads[i].start()

    @pl.when(inner)
    def _():
        pl.semaphore_signal(barrier, inc=1, device_id=across, device_id_type=MESH)
        pl.semaphore_wait(barrier, 5)

    @pl.when(outer)
    def _():
        pl.semaphore_wait(barrier, 4)

    cot_copy = pltpu.make_async_remote_copy(
        src_ref=cot.at[xi], dst_ref=cot.at[xi], send_sem=xs_sem.at[0, 0], recv_sem=xr_sem.at[0, 0],
        device_id=peer, device_id_type=MESH)
    cot_copy.start()

    sums[...] = jnp.zeros_like(sums)
    fsum[...] = jnp.zeros_like(fsum)
    hsum[...] = jnp.zeros_like(hsum)

    def mine(j):
        return pl.multiple_of(j * CH + ci * R, R)

    def mates(j):
        return pl.multiple_of(j * CH + (1 - ci) * R, R)

    def head_mask(h):
        lane = lax.broadcasted_iota(jnp.int32, (8, HC), 1)
        return jnp.where(lane // HEAD_DIM == h, 1.0, 0.0)[0:1].astype(BF16)

    def project(src, w, wi, bias, dst, r0, n, scale=None):
        @pl.loop(0, n // R, unroll=True)
        def _(i):
            r = pl.multiple_of(r0 + i * R, R)
            y = mm(src[pl.ds(r, R), :], w[wi])
            if bias is not None:
                y = y + bias.astype(F32)
            y = y.astype(BF16)
            if scale is not None:
                y = y * jnp.asarray(scale, BF16)
            dst[pl.ds(r, R), :] = y

    SC = 1.0 / math.sqrt(HEAD_DIM)

    def visible(keys_first, r0, nk):
        if keys_first:
            shape, kd = (nk, R), 0
        else:
            shape, kd = (R, nk), 1
        key = lax.broadcasted_iota(jnp.int32, shape, kd)
        row = lax.broadcasted_iota(jnp.int32, shape, 1 - kd) + r0
        return (key <= row) | (key < prefix_ref[0])

    def attend(q, k, v, c, lse, j, causal):
        for i in range(CH // R):
            r0 = j * CH + i * R
            nk = max(T // 2, r0 + R) if causal else T
            rows = slice(r0, r0 + R)
            lane = lax.broadcasted_iota(jnp.int32, (R, 128), 1)
            for h in range(H):
                m = head_mask(h)
                s = mm(q[rows, :] * m, k[:nk, :], NT)
                if causal:
                    s = jnp.where(visible(False, r0, nk), s, MASKED)
                top = jnp.max(s, axis=1, keepdims=True)
                e = jnp.exp(s - top)
                tot = jnp.sum(e, axis=1, keepdims=True)
                p = (e * (1.0 / tot)).astype(BF16)
                o = mm(p, v[:nk, :] * m)
                l = top + jnp.log(tot)
                if h == 0:
                    dqT[...] = o
                    stat = jnp.where(lane == h, l, 0.0)
                else:
                    dqT[...] += o
                    stat = jnp.where(lane == h, l, stat)
            c[rows, :] = dqT[...].astype(BF16)
            lse[:, rows] = jnp.transpose(stat)[0:8, :]

    def attend_back(q, k, v, lse, j, causal, dk, dv, first, slot):
        pbuf, sbuf = act, dpre
        for i in range(CH // R):
            r0 = j * CH + i * R
            nk = max(T // 2, r0 + R) if causal else T
            rows = slice(r0, r0 + R)

            @pl.loop(0, H, unroll=4)
            def _(h):
                m = head_mask(h)
                qh = q[rows, :] * m
                doh = up[i * R:(i + 1) * R, :] * m
                cols = pl.ds(pl.multiple_of(h * R, R), R)
                qm[cols, :] = qh
                dom[cols, :] = doh
                s = mm(k[:nk, :], qh, NT)
                if causal:
                    s = jnp.where(visible(True, r0, nk), s, MASKED)
                p = jnp.exp(s - lse[pl.ds(h, 1), rows])
                dpv = mm(v[:nk, :], doh, NT)
                dd = jnp.sum(p * dpv, axis=0, keepdims=True)
                ds = (p * (dpv - dd)).astype(BF16)
                pbuf[:nk, cols] = p.astype(BF16)
                sbuf[:nk, cols] = ds
                hr = pl.ds(pl.multiple_of(h * HEAD_DIM, HEAD_DIM), HEAD_DIM)
                dqT[hr, :] = mm(kT[hr, :nk], ds)

            @pl.loop(0, nk // R, unroll=True)
            def _(kt):
                kr = pl.ds(pl.multiple_of(kt * R, R), R)
                a = mm(pbuf[kr, :], dom[...])
                b = mm(sbuf[kr, :], qm[...])
                if first and i == 0:
                    dv[kr, :] = a
                    dk[kr, :] = b
                else:
                    dv[kr, :] += a
                    dk[kr, :] += b

            if first and i == 0 and nk < T:
                dv[nk:, :] = jnp.zeros((T - nk, HC), F32)
                dk[nk:, :] = jnp.zeros((T - nk, HC), F32)
            dq = jnp.transpose(dqT[...]) * SC
            hsum[slot] += fold(dq)
            dql[rows, :] = dq.astype(BF16)
            tick()

    def finish_back(dk, dv, slot):
        @pl.loop(0, T // R)
        def _(i):
            r = pl.ds(pl.multiple_of(i * R, R), R)
            a = dv[r, :]
            hsum[slot + 1] += fold(a)
            dvl[r, :] = a.astype(BF16)
            dkl[r, :] = dk[r, :].astype(BF16)

    def sent(s, j):
        return d2l.at[pl.ds(j * R, R)] if s > 5 else chip_send

    def kept(s, j):
        return n2.at[j] if s > 5 else acc

    def chip_copy(s, j):
        dst = mlow.at[pl.ds(j * R, R)] if s == 7 else chip_recv.at[j]
        return pltpu.make_async_remote_copy(
            src_ref=sent(s, j), dst_ref=dst, send_sem=cs_sem.at[s, j], recv_sem=cr_sem.at[s, j],
            device_id=mate, device_id_type=MESH)

    def x_copy(s, j):
        return pltpu.make_async_remote_copy(
            src_ref=x_send.at[j], dst_ref=x_recv.at[s % 2, j], send_sem=xs_sem.at[s, j], recv_sem=xr_sem.at[s, j],
            device_id=peer, device_id_type=MESH)

    def low_copy(s, j, low):
        rows = pl.ds(mine(j), R)
        return pltpu.make_async_remote_copy(
            src_ref=low.at[rows], dst_ref=low.at[rows], send_sem=as_sem.at[s, j], recv_sem=ar_sem.at[s, j],
            device_id=mate, device_id_type=MESH)

    NTILE = 1024

    def partial(s, j, terms):
        send, own = sent(s, j), kept(s, j)

        def tile(r, n):
            y = None
            for lhs, rhs, dims in terms:
                t = mm(lhs[pl.ds(r, R), :], rhs(n), dims)
                y = t if y is None else y + t
            return y

        @pl.loop(0, D // NTILE)
        def _(n):
            n = pl.ds(pl.multiple_of(n * NTILE, NTILE), NTILE)
            send[:, n] = tile(mates(j), n).astype(BF16)

        chip_copy(s, j).start()

        @pl.loop(0, D // NTILE)
        def _(n):
            n = pl.ds(pl.multiple_of(n * NTILE, NTILE), NTILE)
            own[:, n] = tile(mine(j), n)

    RT = 32

    def chip_sum(s, j):
        chip_copy(s, j).wait()

        @pl.loop(0, R // RT, unroll=2)
        def _(i):
            r = pl.ds(pl.multiple_of(i * RT, RT), RT)
            x_send[j, r, :] = (acc[r, :] + chip_recv[j, r, :].astype(F32)).astype(BF16)

        x_copy(s, j).start()

    def total(s, j, r):
        return x_send[j, r, :].astype(F32) + x_recv[s % 2, j, r, :].astype(F32)

    def gain(i):
        return norm_ref[i:i + 1, :]

    def shift(i):
        return norm_ref[3 + i:4 + i, :]

    def obias(i):
        return norm_ref[6 + i:7 + i, :]

    def normed(v):
        cen = v - jnp.mean(v, axis=-1, keepdims=True)
        inv = lax.rsqrt(jnp.mean(cen * cen, axis=-1, keepdims=True) + EPS)
        return cen * inv, inv

    def norm_back(dy, n, inv, i):
        g = dy * gain(i)
        dv = inv * (g - jnp.mean(g, axis=-1, keepdims=True) - n * jnp.mean(g * n, axis=-1, keepdims=True))
        sums[i] += fold(dy * n)
        sums[3 + i] += fold(dy)
        sums[6 + i] += fold(dv)
        return dv

    def finish(s, j, low):
        x_copy(s, j).wait()
        base = mine(j)

        @pl.loop(0, R // RT, unroll=2)
        def _(i):
            r = pl.ds(pl.multiple_of(i * RT, RT), RT)
            g = pl.ds(pl.multiple_of(base + i * RT, RT), RT)
            t = total(s, j, r)
            if s == 1:
                n, inv = normed(xin[g, :].astype(F32) + t + obias(0))
                n1[j, r, :] = n
                inv1[j, r, :] = jnp.broadcast_to(inv, (RT, 128))
                low[g, :] = (n * gain(0) + shift(0)).astype(BF16)
            elif s == 2:
                n, inv = normed(n1[j, r, :] * gain(0) + shift(0) + t + obias(1))
                n2[j, r, :] = n
                inv2[j, r, :] = jnp.broadcast_to(inv, (RT, 128))
                low[g, :] = (n * gain(1) + shift(1)).astype(BF16)
            elif s == 3:
                n, inv = normed(n2[j, r, :] * gain(1) + shift(1) + t + obias(2))
                dy = cot[j, r, :].astype(F32)
                obuf[j, r, :] = (n * gain(2) + shift(2)).astype(BF16)
                d = norm_back(dy, n, inv, 2)
                dcur[j, r, :] = d
                low[g, :] = d.astype(BF16)
            elif s == 4:
                d = norm_back(dcur[j, r, :] + t, n2[j, r, :], inv2[j, r, 0:1], 1)
                dcur[j, r, :] = d
                low[g, :] = d.astype(BF16)
            else:
                d = norm_back(dcur[j, r, :] + t, n1[j, r, :], inv1[j, r, 0:1], 0)
                dcur[j, r, :] = d
                low[g, :] = d.astype(BF16)

        low_copy(s, j, low).start()

    def gather(s, j, low):
        low_copy(s, j, low).wait()

    def got(s, j, i):
        if s == 7:
            return mlow[pl.ds(pl.multiple_of(j * R + i * RT, RT), RT), :].astype(F32)
        return chip_recv[j, pl.ds(pl.multiple_of(i * RT, RT), RT), :].astype(F32)

    def scatter_send(s):
        for j in range(2):
            chip_copy(s, j).wait()
        j = 1 - xi

        @pl.loop(0, R // RT, unroll=2)
        def _(i):
            r = pl.ds(pl.multiple_of(i * RT, RT), RT)
            x_send[0, r, :] = (n2[j, r, :] + got(s, j, i)).astype(BF16)

        x_copy(s, 0).start()

    def scatter_finish(s, extra, dst):
        x_copy(s, 0).wait()

        @pl.loop(0, R // RT, unroll=2)
        def _(i):
            r = pl.ds(pl.multiple_of(i * RT, RT), RT)
            t = n2[xi, r, :] + got(s, xi, i) + x_recv[s % 2, 0, r, :].astype(F32)
            if extra is not None:
                t = t + extra[xi, r, :]
            dst[r, :] = t.astype(BF16)

    def grad_rows(u, lhs, c0, rhs):
        @pl.loop(0, D // NTILE)
        def _(n):
            n = pl.ds(pl.multiple_of(n * NTILE, NTILE), NTILE)
            unit, r0 = units[u]
            unit[r0:r0 + R, n] = mm(lhs[:, pl.ds(c0, R)], rhs[:, n], TN).astype(BF16)

    def grad_cols(pairs, lhs):
        @pl.loop(0, D // R, unroll=True)
        def _(b):
            cols = pl.ds(pl.multiple_of(b * R, R), R)
            for u, rhs in pairs:
                unit, r0 = units[u]
                unit[r0:r0 + R, cols] = mm(lhs[:, cols], rhs[...], TN).astype(BF16)


    Q = R // 4

    def ring_rows(u, at, n=Q):
        return ring.at[pl.ds((u % SLOTS) * 8 * Q + at * Q, n)]

    def hop(u, i):
        ref, r0 = units[u]
        k = u % SLOTS

        def rows(at):
            return ref.at[pl.ds(pl.multiple_of(r0 + at * Q, Q), Q)]

        hz = zi // 2
        if i == "a1":
            n, src, dst, dev = 0, rows(1 - yi), ring_rows(u, 0), ymate
        elif i == "a2":
            n, src, dst, dev = 1, rows(yi), ring_rows(u, 1), zmate
        elif i == "a3":
            n, src, dst, dev = 2, rows(yi), ring_rows(u, 7), across
        elif i == "a4":
            n, src, dst, dev = 3, rows(yi), ring_rows(u, 1), zmate
        elif i == "a5i":
            n, src, dst, dev = 4, rows(yi), ring_rows(u, 2), ymate
        elif i == "a5o":
            n, src, dst, dev = 4, ring_rows(u, 1), ring_rows(u, 2), ymate
        elif i == "b1":
            n, src, dst, dev = 5, ref.at[pl.ds(r0 + 2 * Q, 2 * Q)], ring_rows(u, 6, 2 * Q), zmate
        elif i == "b2":
            n, src, dst, dev = 6, rows(2 + 1 - hz), ring_rows(u, 3), across
        elif i == "b3":
            n, src, dst, dev = 7, rows(2 + hz), ring_rows(u, 4), ymate
        elif i == "b4":
            n, src, dst, dev = 8, rows(2 + hz), ring_rows(u, 5), across
        elif i == "b5o":
            n, src, dev = 9, rows(2 + hz), zmate
            dst = ring.at[pl.ds(pl.multiple_of(k * 8 * Q + (6 + hz) * Q, Q), Q)]
        elif i == "b5t":
            n, src, dev = 10, ring_rows(u, 5), zmate
            dst = ring.at[pl.ds(pl.multiple_of(k * 8 * Q + (7 - hz) * Q, Q), Q)]
        return pltpu.make_async_remote_copy(
            src_ref=src, dst_ref=dst, send_sem=ds_sem.at[k, n], recv_sem=dr_sem.at[k, n],
            device_id=dev, device_id_type=MESH)

    def add(u, row, at, n):
        ref, r0 = units[u]
        base = (u % SLOTS) * 8 * Q + at * Q

        @pl.loop(0, n // 16)
        def _(i):
            a = pl.ds(pl.multiple_of(r0 + row * Q + i * 16, 16), 16)
            b = pl.ds(pl.multiple_of(base + i * 16, 16), 16)
            ref[a, :] = (ref[a, :].astype(F32) + ring[b, :].astype(F32)).astype(BF16)

    def store(u, i, src, row, n=Q):
        sem = do_sem.at[u % SLOTS, i]

        def rows(base):
            return pl.ds(pl.multiple_of(base + row * Q, Q), n)

        if u < 8:
            whole = (g2_hbm if u < 4 else g1_hbm).at[rows(u % 4 * R)]
        elif u % 4 == 0:
            whole = (gco_hbm if u == 8 else gso_hbm).at[rows(0)]
        else:
            dst = (gcq_hbm if u < 12 else gsq_hbm).at[u % 4 - 1]
            return [pltpu.make_async_copy(src.at[:, pl.ds(b * R, R)], dst.at[rows(b * R)], do_sem.at[u % SLOTS, 4 * b + i])
                    for b in range(D // R)]
        return [pltpu.make_async_copy(src, whole, sem)]

    def stores(u):
        ref, r0 = units[u]
        hz = zi // 2

        def rows(at):
            return ref.at[pl.ds(pl.multiple_of(r0 + at * Q, Q), Q)]

        both = store(u, 0, ring_rows(u, 2), 1 - yi)
        if_inner = store(u, 1, rows(yi), yi) + store(u, 2, rows(2 + hz), 2 + hz) + store(u, 3, ring_rows(u, 5), 3 - hz)
        if_outer = store(u, 1, ring_rows(u, 1), yi) + store(u, 2, ring_rows(u, 6, 2 * Q), 2, 2 * Q)
        return both, if_inner, if_outer

    def advance(u, stage):
        hz = zi // 2
        if stage == 0:
            hop(u, "a1").start()

            @pl.when(outer)
            def _():
                hop(u, "b1").start()
        elif stage == 1:
            hop(u, "a1").wait()
            add(u, yi, 0, Q)

            @pl.when(outer)
            def _():
                hop(u, "a2").start()
                hop(u, "b1").wait_send()

            @pl.when(inner)
            def _():
                hop(u, "b1").wait_recv()
                add(u, 2, 6, 2 * Q)
                hop(u, "b2").start()
        elif stage == 2:
            @pl.when(outer)
            def _():
                hop(u, "a2").wait_send()

            @pl.when(inner)
            def _():
                hop(u, "b2").wait()
                add(u, 2 + hz, 3, Q)
                hop(u, "b3").start()
                hop(u, "a2").wait_recv()
                add(u, yi, 1, Q)
                hop(u, "a3").start()
        elif stage == 3:
            @pl.when(inner)
            def _():
                hop(u, "a3").wait()
                add(u, yi, 7, Q)
                hop(u, "a4").start()
                hop(u, "a5i").start()
                hop(u, "b3").wait()
                add(u, 2 + hz, 4, Q)
                hop(u, "b4").start()
                hop(u, "b5o").start()
        elif stage == 4:
            @pl.when(inner)
            def _():
                hop(u, "b4").wait()
                hop(u, "b5t").start()

            @pl.when(outer)
            def _():
                hop(u, "a4").wait_recv()
                hop(u, "a5o").start()
        elif stage == 5:
            both, if_inner, if_outer = stores(u)

            @pl.when(inner)
            def _():
                hop(u, "a5i").wait()
                for c in if_inner:
                    c.start()

            @pl.when(outer)
            def _():
                hop(u, "a5o").wait()
                hop(u, "b5o").wait_recv()
                hop(u, "b5t").wait_recv()
                for c in if_outer:
                    c.start()

            for c in both:
                c.start()
        else:
            both, if_inner, if_outer = stores(u)
            for c in both:
                c.wait()

            @pl.when(inner)
            def _():
                for i in ("a4", "b5o", "b5t"):
                    hop(u, i).wait_send()
                for c in if_inner:
                    c.wait()

            @pl.when(outer)
            def _():
                for c in if_outer:
                    c.wait()

    def small_hop(i):
        dev = (mate, ymate, zmate, across, zmate)[i]
        return pltpu.make_async_remote_copy(
            src_ref=small_ref, dst_ref=sring.at[2 if i == 4 else i], send_sem=ss_sem.at[i],
            recv_sem=sr_sem.at[i], device_id=dev, device_id_type=MESH)

    def advance_small(stage):
        if stage == 0:
            for i in range(9):
                small_ref[i:i + 1, :] = jnp.sum(sums[i], axis=0, keepdims=True)
            small_ref[9:10, :] = jnp.sum(fsum[...], axis=0, keepdims=True)
            for i in range(4):
                small_ref[10:11, i * HC:(i + 1) * HC] = jnp.sum(hsum[i], axis=0, keepdims=True)
            small_ref[11:16, :] = jnp.zeros((5, D), F32)
            small_hop(0).start()
        elif stage == 1:
            small_hop(0).wait()
            small_ref[0:9, :] += sring[0, 0:9, :]
            small_hop(1).start()
        elif stage == 2:
            small_hop(1).wait()
            small_ref[...] += sring[1]

            @pl.when(outer)
            def _():
                small_hop(2).start()
        elif stage == 3:
            @pl.when(outer)
            def _():
                small_hop(2).wait_send()

            @pl.when(inner)
            def _():
                small_hop(2).wait_recv()
                small_ref[...] += sring[2]
                small_hop(3).start()
        elif stage == 4:
            @pl.when(inner)
            def _():
                small_hop(3).wait()
                small_ref[...] += sring[3]
                small_hop(4).start()
        elif stage == 5:
            @pl.when(inner)
            def _():
                small_hop(4).wait_send()

            @pl.when(outer)
            def _():
                small_hop(4).wait_recv()
                small_ref[...] = sring[2]

    ready, flight, lag = [], [], list(LAG)

    def launch(n=1):
        new = []
        while n and ready and (ready[0] == "small" or len(flight) + len(new) < SLOTS):
            u = ready.pop(0)
            if u == "small":
                advance_small(0)
            else:
                advance(u, 0)
            new.append([u, 1, lag[1]])
            n -= 1
        return new

    def start(n=1):
        flight.extend(launch(n))

    def step(item):
        item[2] -= 1
        if item[2] > 0:
            return
        if item[0] == "small":
            advance_small(item[1])
        else:
            advance(item[0], item[1])
        item[1] += 1
        item[2] = lag[item[1] % 7]

    def tick(n=1):
        for item in [i for i in flight if i[1] == 6]:
            step(item)
            if item[1] == 7:
                flight.remove(item)
        new = launch(n)
        for item in flight:
            if item[1] < 6:
                step(item)
        flight.extend(new)

    loads[XIN].wait()
    loads[WSQ].wait()
    for i in (WSO, MEMR, WCQ, WCO, W1, W2):
        loads[i].start()
    project(xin, wsq, 0, sbias_ref[0:1, :], q1, 0, T, SC)
    project(xin, wsq, 1, None, k1, 0, T)
    project(xin, wsq, 2, sbias_ref[1:2, :], v1, 0, T)
    loads[WSO].wait()

    def self_forward(j):
        attend(q1, k1, v1, c1, lse1, j, True)
        partial(1, j, [(c1, lambda n: wso[:, n], NN)])
        chip_sum(1, j)

    def cross_forward(j):
        project(mlow, wcq, 0, cbias_ref[0:1, :], q2, j * CH, CH, SC)
        attend(q2, k2, v2, c2, lse2, j, False)
        partial(2, j, [(c2, lambda n: wco[:, n], NN)])
        chip_sum(2, j)

    def ffn_forward(j):
        @pl.loop(0, CH // R)
        def _(i):
            r = pl.ds(pl.multiple_of(j * CH + i * R, R), R)

            @pl.loop(0, FF // 256, unroll=4)
            def _(n):
                cols = pl.ds(pl.multiple_of(n * 256, 256), 256)
                pre = mm(slow[r, :], w1[:, cols]) + norm_ref[9:10, cols]
                half = 0.5 * (1.0 + lax.erf(pre * (1.0 / math.sqrt(2.0))))
                act[r, cols] = (pre * half).astype(BF16)
                slope[n, r, :] = half + pre * jnp.exp(-0.5 * pre * pre) * (1.0 / math.sqrt(2.0 * math.pi))

        partial(3, j, [(act, lambda n: w2[:, n], NN)])
        chip_sum(3, j)

    def ffn_backward(j):
        @pl.loop(0, CH // R)
        def _(i):
            r = pl.ds(pl.multiple_of(j * CH + i * R, R), R)

            @pl.loop(0, FF // 256, unroll=4)
            def _(n):
                cols = pl.ds(pl.multiple_of(n * 256, 256), 256)
                t = mm(d3l[r, :], w2[cols, :], NT) * slope[n, r, :]
                fsum[:, cols] += fold(t)
                dpre[r, cols] = t.astype(BF16)

        partial(4, j, [(dpre, lambda n: w1[n, :], NT)])
        chip_sum(4, j)

    self_forward(0)
    self_forward(1)
    loads[MEMR].wait()
    loads[WCQ].wait()
    project(mem, wcq, 1, None, k2, 0, T)
    project(mem, wcq, 2, cbias_ref[1:2, :], v2, 0, T)
    loads[WCO].wait()
    finish(1, 0, mlow)
    gather(1, 0, mlow)
    cross_forward(0)
    finish(1, 1, mlow)
    gather(1, 1, mlow)
    cross_forward(1)
    loads[W1].wait()
    loads[W2].wait()
    finish(2, 0, slow)
    gather(2, 0, slow)
    ffn_forward(0)
    finish(2, 1, slow)
    gather(2, 1, slow)
    ffn_forward(1)
    cot_copy.wait()
    finish(3, 0, d3l)
    gather(3, 0, d3l)
    ffn_backward(0)
    finish(3, 1, d3l)
    gather(3, 1, d3l)
    for u in range(2):
        grad_rows(u, act, u * R, d3l)
        ready.append(u)
        if u == 0:
            start()
    ffn_backward(1)
    out_copy = pltpu.make_async_copy(obuf.at[xi], out_hbm, out_sems.at[0])
    out_copy.start()
    tick()
    for u in range(2, 4):
        grad_rows(u, act, u * R, d3l)
        ready.append(u)
    for u in range(4):
        grad_rows(4 + u, slow, u * R, dpre)
        ready.append(4 + u)
    tick()
    out_copies = [out_copy]

    def emit(i, src, dst):
        c = pltpu.make_async_copy(src, dst, out_sems.at[i])
        c.start()
        out_copies.append(c)

    def upstream(low, wo, j):
        @pl.loop(0, CH // R, unroll=True)
        def _(i):
            r = pl.ds(pl.multiple_of(j * CH + i * R, R), R)
            up[pl.ds(pl.multiple_of(i * R, R), R), :] = mm(low[r, :], wo[...], NT).astype(BF16)

    dk, dv = slope.at[0], slope.at[1]

    def cross_backward(j):
        upstream(d2l, wco, j)
        attend_back(q2, k2, v2, lse2, j, False, dk, dv, j == 0, 2)
        partial(5, j, [(dql, lambda n: wcq[0, n, :], NT)])
        tick()
        chip_sum(5, j)

    def self_backward(j):
        upstream(d1l, wso, j)
        attend_back(q1, k1, v1, lse1, j, True, dk, dv, j == 0, 0)

    kT[...] = jnp.transpose(k2[...])
    finish(4, 0, d2l)
    tick()
    gather(4, 0, d2l)
    cross_backward(0)
    finish(4, 1, d2l)
    tick()
    gather(4, 1, d2l)
    grad_rows(8, c2, 0, d2l)
    ready.append(8)
    cross_backward(1)
    finish_back(dk, dv, 2)
    grad_cols([(9, dql)], mlow)
    grad_cols([(10, dkl), (11, dvl)], mem)
    x_again = pltpu.make_async_copy(x_hbm, mem, in_sems.at[0])
    x_again.start()
    ready.extend([9, 10, 11])
    tick()

    kT[...] = jnp.transpose(k1[...])
    d1l = d3l
    finish(5, 0, d1l)
    tick()
    gather(5, 0, d1l)
    self_backward(0)
    finish(5, 1, d1l)
    tick()
    gather(5, 1, d1l)
    grad_rows(12, c1, 0, d1l)
    ready.append(12)
    for j in range(2):
        partial(6, j, [(dkl, lambda n: wcq[1, n, :], NT), (dvl, lambda n: wcq[2, n, :], NT)])
    tick()
    scatter_send(6)
    self_backward(1)
    scatter_finish(6, None, mem_out := obuf.at[1 - xi])
    emit(1, mem_out, mg_hbm)
    finish_back(dk, dv, 0)
    x_again.wait()
    grad_cols([(13, dql), (14, dkl), (15, dvl)], mem)
    ready.extend([13, 14, 15, "small"])
    lag[:] = LAST
    tick()
    for j in range(2):
        partial(7, j, [(dql, lambda n: wsq[0, n, :], NT), (dkl, lambda n: wsq[1, n, :], NT),
                       (dvl, lambda n: wsq[2, n, :], NT)])
    tick()
    scatter_send(7)
    for _ in range(4):
        tick()
    out_copy.wait()
    scatter_finish(7, dcur, obuf.at[xi])
    emit(2, obuf.at[xi], ig_hbm)
    while ready or flight:
        tick()
    for c in out_copies[1:]:
        c.wait()


def shards(inputs, memory, prefix, self_qkv, self_bias, self_out, cross_qkv, cross_bias, cross_out,
           ffn_in, ffn_in_bias, ffn_out, norm_gain, norm_shift, out_bias, cotangent):
    T, D = inputs.shape
    HC = self_out.shape[0]
    FF = ffn_out.shape[0]
    R = T // 4
    norms = jnp.concatenate(
        [norm_gain.T, norm_shift.T, out_bias.T, ffn_in_bias[None, :], jnp.zeros((6, D), BF16)], axis=0).astype(F32)
    sds = jax.ShapeDtypeStruct
    v = pltpu.VMEM
    dma = pltpu.SemaphoreType.DMA
    outs = pl.pallas_call(
        functools.partial(layer_kernel, T, D, HC, FF),
        out_shape=(
            sds((R, D), BF16), sds((R, D), BF16), sds((R, D), BF16),
            sds((3, D, HC), BF16), sds((HC, D), BF16), sds((3, D, HC), BF16), sds((HC, D), BF16),
            sds((D, FF), BF16), sds((FF, D), BF16), sds((16, D), F32),
        ),
        in_specs=[ANY, ANY, SMEM] + [ANY] * 7 + [VMEM] * 3,
        out_specs=(ANY,) * 9 + (VMEM,),
        scratch_shapes=[
            v((T, D), BF16), v((T, D), BF16), v((3, D, HC), BF16), v((HC, D), BF16), v((3, D, HC), BF16),
            v((HC, D), BF16), v((D, FF), BF16), v((FF, D), BF16), v((2, R, D), BF16),
        ] + [v((T, HC), BF16)] * 8 + [v((8, T), F32)] * 2 + [
            v((T, D), BF16), v((T, D), BF16), v((T, D), BF16), v((T, D), BF16),
            v((T, FF), BF16), v((FF // 256, T, 256), F32), v((T, FF), BF16),
            v((2, R, D), F32), v((2, R, D), F32), v((2, R, 128), F32), v((2, R, 128), F32), v((2, R, D), F32),
            v((R, D), BF16), v((2, R, D), BF16), v((R, D), F32), v((2, R, D), BF16), v((2, 2, R, D), BF16),
            v((T, HC), BF16), v((T, HC), BF16), v((T, HC), BF16), v((HC, T), BF16), v((HC, R), F32),
            v((4 * R, HC), BF16), v((4 * R, HC), BF16), v((T // 2, HC), BF16), v((SLOTS * 2 * R, D), BF16), v((4, 16, D), F32),
            v((9, 8, D), F32), v((8, FF), F32), v((4, 8, HC), F32),
            dma((9,)), dma((4,)), dma((8, 2)), dma((8, 2)), dma((8, 2)), dma((8, 2)), dma((8, 2)), dma((8, 2)),
            dma((SLOTS, 11)), dma((SLOTS, 11)), dma((SLOTS, 16)), dma((5,)), dma((5,)),
        ],
        compiler_params=pltpu.CompilerParams(
            collective_id=0, has_side_effects=True, vmem_limit_bytes=64 * 2**20 - 256 * 1024),
    )(inputs, memory, prefix, self_qkv, self_out, cross_qkv, cross_out, ffn_in, ffn_out, cotangent,
      norms, self_bias, cross_bias)
    out, ig, mg = outs[:3]
    grads, small = outs[3:9], outs[9]
    count = lax.axis_size("dp")
    if count > 8:
        same = [[g * 8 + i for g in range(count // 8)] for i in range(8)]
        grads, small = lax.psum((grads, small), "dp", axis_index_groups=same)
    gsq, gso, gcq, gco, g1, g2 = [g.astype(F32) for g in grads]
    share = D // lax.axis_size("tensor")
    rows = lax.dynamic_slice_in_dim(small[:9], lax.axis_index("tensor") * share, share, 1).T
    hb = small[10].reshape(4, HC)
    return (out, ig, mg, gsq, hb[0:2], gso, gcq, hb[2:4], gco, g1, small[9], g2,
            rows[:, 0:3], rows[:, 3:6], rows[:, 6:9])


def solution(mesh):
    t = "tensor"
    return jax.shard_map(
        shards,
        mesh=mesh,
        in_specs=(
            P("dp", None), P("dp", None), P("dp"), P(None, None, t), P(None, t), P(t, None), P(None, None, t),
            P(None, t), P(t, None), P(None, t), P(t), P(t, None), P(), P(), P(), P(("dp", t), None),
        ),
        out_specs=(
            P(("dp", t), None), P(("dp", t), None), P(("dp", t), None), P(None, None, t), P(None, t), P(t, None),
            P(None, None, t), P(None, t), P(t, None), P(None, t), P(t), P(t, None), P(t, None), P(t, None),
            P(t, None),
        ),
        check_vma=False,
    )
```
